512 devices in a mesh: span: 8 (over x, y_lo), seq: 64 (over y_hi, z, core).
Axes of the slice: x: 4, y: 8 (y_hi: 4, y_lo: 2; y = y_hi * 2 + y_lo), z: 8, core: 2. Of those that a mesh axis runs over, the one named last changes fastest.
Arguments:
- queries: bfloat16 [4096, 8192], P(('span', 'seq')), may hold values from -100 to 100
- keys: bfloat16 [4096, 8192], P(('span', 'seq')), may hold values from -6 to 6
- values: bfloat16 [4096, 8192], P(('span', 'seq')), may hold values from -24 to 24
- context: bfloat16 [2, 1024, 8192], P(None, 'span', 'seq'), may hold values from -12 to 12
- gate_table: float32 [64, 8192], P(None, 'seq'), may hold values from 0.1 to 1.9
- order: int32 [8], replicated, may hold values from 0 to 7, each once
- noise_step: int32 [8], replicated, may hold values from 0 to 63
- ctx_mask: int32 [8, 1024], replicated, may hold values from 0 to 1
Outputs:
- attended: bfloat16 [4096, 8192], P(('span', 'seq'))
The draws below stay inside these ranges and needn't reach their ends.
All inputs are finite; a program needn't handle non-finite values.
Results may differ from the reference program's by a relative error of at most 0.004.
Values may be sent and summed in bfloat16 or wider, within the bound.
A program may use at most 64 MiB of HBM per device.

```python
import jax
import jax.numpy as jnp
from jax import lax

HD = 128
STEPS = 64
HEADS = 64
SPAN_LEN = 512
TOKENS = 4096
CTX = 1024
N_SPAN = 8


def shared_keys(key):
    base = jax.random.normal(jax.random.fold_in(key, 101), (TOKENS, HEADS * HD), jnp.float32)
    return jnp.clip(base, -6.0, 6.0)


def draw_queries(key, part):
    key = jax.random.fold_in(key, 3)
    drawn = jnp.clip(2.0 * jax.random.normal(key, (TOKENS, HEADS * HD), jnp.float32), -12.0, 12.0)
    return drawn.astype(jnp.bfloat16)


def draw_keys(key, part):
    key_base = shared_keys(key)
    return key_base.astype(jnp.bfloat16)


def draw_ctx_mask(key, part):
    key = jax.random.fold_in(key, 7)
    picks = jax.random.randint(key, (N_SPAN, CTX), 0, 4, dtype=jnp.int32)
    return jnp.where(picks > 0, 1, 0).astype(jnp.int32)


def with_ends(entries, own_key, low, high):
    place = [jax.random.randint(jax.random.fold_in(own_key, axis), (), 0, length) for axis, length in enumerate(entries.shape)]
    longest = entries.shape.index(max(entries.shape))
    beside = place[:longest] + [(place[longest] + 1) % entries.shape[longest]] + place[longest + 1:]
    return entries.at[tuple(place)].set(low).at[tuple(beside)].set(high)


def levels(key, shape, shards, low, top_value):
    loudness = 1.0
    for axis_at, parts in shards:
        heights = jax.random.uniform(jax.random.fold_in(jax.random.fold_in(key, 6), axis_at), (parts,), jnp.float32, low / len(shards), top_value / len(shards))
        loudness = loudness * jnp.repeat(jnp.exp(heights), shape[axis_at] // parts).reshape((-1,) + (1,) * (len(shape) - 1 - axis_at))
    return loudness


def centred(stream_key, extent, deviation, reach, split=(), kind=jnp.bfloat16):
    factor_of = levels(stream_key, extent, split, -0.22, 0.18) if split else 1.0
    drawn = jax.random.normal(stream_key, extent, jnp.float32) * deviation * factor_of
    return jnp.minimum(jnp.maximum(drawn, -reach), reach).astype(kind)


def setup_inputs(seed: int = 0) -> dict:
    key_of = jax.random.split(jax.random.key(seed), 9)
    return {
        "queries": draw_queries(jax.random.fold_in(key_of[8], 71), 0),
        "keys": draw_keys(jax.random.fold_in(key_of[8], 71), 0),
        "values": centred(key_of[2], (TOKENS, HEADS * HD), 4.0, 24.0, ((0, 512),)),
        "context": centred(key_of[3], (2, CTX, HEADS * HD), 2.0, 12.0, ((1, 8), (2, 64))),
        "gate_table": jnp.clip(1.0 + 0.18 * jax.random.normal(key_of[4], (STEPS, HEADS * HD), jnp.float32), 0.1, 1.9),
        "order": jax.random.permutation(key_of[5], N_SPAN).astype(jnp.int32),
        "noise_step": with_ends(jax.random.randint(key_of[6], (N_SPAN,), 0, STEPS), jax.random.fold_in(key_of[6], 1), 0, STEPS - 1).astype(jnp.int32),
        "ctx_mask": draw_ctx_mask(jax.random.fold_in(key_of[8], 71), 0),
    }


NEG_FILL = -1e30


def reference(queries, keys, values, context, gate_table, order, noise_step, ctx_mask):
    score_factor = HD ** -0.5
    row_span = (jnp.arange(TOKENS, dtype=jnp.int32) // SPAN_LEN).astype(jnp.int32)

    def one_head(flat_index):
        span_id = (flat_index // HEADS).astype(jnp.int32)
        head_id = (flat_index % HEADS).astype(jnp.int32)
        column = (head_id * HD).astype(jnp.int32)
        query_rows = lax.dynamic_slice(queries, ((span_id * SPAN_LEN).astype(jnp.int32), column), (SPAN_LEN, HD))
        key_cols = lax.dynamic_slice_in_dim(keys, column, HD, 1)
        value_cols = lax.dynamic_slice_in_dim(values, column, HD, 1)
        ctx_keys = lax.dynamic_slice_in_dim(context[0], column, HD, 1)
        ctx_values = lax.dynamic_slice_in_dim(context[1], column, HD, 1)
        all_keys = jnp.concatenate([ctx_keys, key_cols], 0)
        all_values = jnp.concatenate([ctx_values, value_cols], 0)
        own_order = order[span_id]
        span_seen = (order[row_span] < own_order) | (row_span == span_id)
        ctx_seen = ctx_mask[span_id] == 1
        visible = jnp.concatenate([ctx_seen, span_seen])
        scores = lax.dot_general(query_rows, all_keys, (((1,), (1,)), ((), ())), preferred_element_type=jnp.float32) * score_factor
        scores = jnp.where(visible[None, :], scores, NEG_FILL)
        row_peak = jnp.max(scores, 1, keepdims=True)
        weights = jnp.where(visible[None, :], jnp.exp(scores - row_peak), 0.0)
        row_total = jnp.sum(weights, 1, keepdims=True)
        mixture = jnp.dot(weights.astype(jnp.bfloat16), all_values, preferred_element_type=jnp.float32) / row_total
        gate_row = lax.dynamic_slice(gate_table, (noise_step[span_id].astype(jnp.int32), column), (1, HD))
        return (mixture * gate_row).astype(jnp.bfloat16)

    blocks = lax.map(one_head, jnp.arange(N_SPAN * HEADS, dtype=jnp.int32))
    return blocks.reshape(N_SPAN, HEADS, SPAN_LEN, HD).transpose(0, 2, 1, 3).reshape(TOKENS, HEADS * HD)
```

```python
import jax
import jax.numpy as jnp
from jax import lax
from jax.experimental import pallas as pl
from jax.experimental.pallas import tpu as pltpu
from jax.sharding import PartitionSpec as P

MESH = pl.DeviceIdType.MESH
NEG_FILL = -1e30
LOG2E = 1.4426950408889634
HD = 128
GROUP_ORDER = (1, 4, 2, 3)


def kernel(q_hbm, k_hbm, v_hbm, ctx_hbm, gate_hbm, order_hbm, step_hbm, mask_hbm, out_ref,
           q_in, k_in, v_in, ctx_in, gate_in, order_s, step_s, mask_in,
           kv_out, ctx_out, kv, q_rows, gate_sib, out_rows, ctx_bias,
           load_sem, own_sem, left_sem, right_sem, far_sem, sib_sem, misc_sem, send_sem):
    span, seq = lax.axis_index("span"), lax.axis_index("seq")
    x, yl = span // 2, span % 2
    yh, z, k = seq // 16, (seq // 2) % 8, seq % 2
    y = yh * 2 + yl
    stays = yl == k
    own = x * 2 + k
    left_x, right_x, far_x = (x + 3) % 4, (x + 1) % 4, (x + 2) % 4

    def device(x_, y_, z_, k_):
        return (x_ * 2 + y_ % 2, (y_ // 2) * 16 + z_ * 2 + k_)

    left, right = device(left_x, y, z, k), device(right_x, y, z, k)
    sibling = device(x, y, z, 1 - k)

    def remote(src, dst, sent, got, to):
        return pltpu.make_async_remote_copy(
            src_ref=src, dst_ref=dst, send_sem=sent, recv_sem=got, device_id=to, device_id_type=MESH
        )

    def wait_for(ref, sem):
        pltpu.make_async_copy(ref, ref, sem).wait()

    def far_first(i):
        return 4 + (1 - 2 * (i % 2)) * ((i + 1) // 2)

    loads = [
        pltpu.make_async_copy(src, dst, load_sem.at[i])
        for i, (src, dst) in enumerate(
            [(k_hbm, k_in), (v_hbm, v_in), (ctx_hbm, ctx_in), (q_hbm, q_in), (gate_hbm, gate_in),
             (order_hbm, order_s), (step_hbm, step_s), (mask_hbm, mask_in)]
        )
    ]
    for load in loads:
        load.start()

    barrier = pltpu.get_barrier_semaphore()

    def greet(j, carry):
        z_, y_, k_ = (z + far_first(j // 8)) % 8, (yh + 2 + (j // 2) % 4) % 4 * 2 + k, j % 2

        @pl.when((z_ != z) | (y_ != y) | (k_ != k))
        def _():
            pl.semaphore_signal(barrier, inc=1, device_id=device(x, y_, z_, k_), device_id_type=MESH)

        return carry

    lax.fori_loop(0, 64, greet, 0)
    for to in (left, right, sibling):
        pl.semaphore_signal(barrier, inc=1, device_id=to, device_id_type=MESH)

    for load in loads[:3]:
        load.wait()
    for h in range(64):
        kv_out[h, 0] = k_in[:, h * HD:(h + 1) * HD]
        kv_out[h, 1] = v_in[:, h * HD:(h + 1) * HD]
    ctx_out[...] = ctx_in[...].reshape(ctx_out.shape)
    for load in loads[3:]:
        load.wait()

    @pl.when(stays)
    def _():
        pl.semaphore_wait(barrier, 66)

    @pl.when(jnp.logical_not(stays))
    def _():
        pl.semaphore_wait(barrier, 67)

    gate_copy = remote(gate_in, gate_sib, misc_sem.at[0], misc_sem.at[1], sibling)
    gate_copy.start()

    @pl.when(stays)
    def _():
        pltpu.make_async_copy(ctx_out, kv.at[:, own, 0], own_sem.at[0]).start()

    @pl.when(jnp.logical_not(stays))
    def _():
        remote(ctx_out, kv.at[:, span, 0], send_sem.at[0], own_sem.at[0], device(x, yh * 2 + k, z, yl)).start()

    def send_group(g):
        def send_one(j, carry):
            z_, y_ = (z + far_first(j // 2)) % 8, (y + 8 - 2 * g - j % 2) % 8
            h = (y_ // 2) * 16 + z_ * 2 + y_ % 2
            dst = kv.at[:, span, 1 + g, z * 2 + k]
            here = stays & (y_ == y) & (z_ == z)

            @pl.when(here)
            def _():
                pltpu.make_async_copy(kv_out.at[h], dst, own_sem.at[1 + g]).start()

            @pl.when(jnp.logical_not(here))
            def _():
                remote(kv_out.at[h], dst, send_sem.at[1], own_sem.at[1 + g], device(x, y_, z_, yl)).start()

            return carry

        lax.fori_loop(0, 16, send_one, 0)

    for slot in GROUP_ORDER:
        send_group(slot - 1)

    def to_sibling(ref, kind):
        remote(ref, ref, send_sem.at[4], sib_sem.at[kind], sibling).start()

    def pass_own(slot):
        ref = kv.at[:, own, slot]
        wait_for(ref, own_sem.at[slot])
        remote(ref, ref, send_sem.at[3], left_sem.at[slot], right).start()
        remote(ref, ref, send_sem.at[3], right_sem.at[slot], left).start()
        to_sibling(ref, 0)

    def pass_near(slot):
        from_left, from_right = kv.at[:, left_x * 2 + k, slot], kv.at[:, right_x * 2 + k, slot]
        wait_for(from_left, left_sem.at[slot])
        half = kv.at[0, left_x * 2 + k, slot]
        remote(half, half, send_sem.at[3], far_sem.at[slot, 0], right).start()
        to_sibling(from_left, 1)
        wait_for(from_right, right_sem.at[slot])
        half = kv.at[1, right_x * 2 + k, slot]
        remote(half, half, send_sem.at[3], far_sem.at[slot, 1], left).start()
        to_sibling(from_right, 2)

    def pass_far(slot):
        ref = kv.at[:, far_x * 2 + k, slot]
        wait_for(kv.at[0, far_x * 2 + k, slot], far_sem.at[slot, 0])
        wait_for(kv.at[1, far_x * 2 + k, slot], far_sem.at[slot, 1])
        to_sibling(ref, 3)

    pass_own(0)

    def send_query(j, carry):
        z_, y_ = (z + far_first(j // 8)) % 8, (y + 4 + j) % 8
        h = (y_ // 2) * 16 + z_ * 2 + y_ % 2
        src = q_in.at[:, pl.ds(pl.multiple_of(h * HD, HD), HD)]
        dst = q_rows.at[seq]
        here = stays & (y_ == y) & (z_ == z)

        @pl.when(here)
        def _():
            pltpu.make_async_copy(src, dst, misc_sem.at[2]).start()

        @pl.when(jnp.logical_not(here))
        def _():
            remote(src, dst, send_sem.at[2], misc_sem.at[2], device(x, y_, z_, yl)).start()

        return carry

    lax.fori_loop(0, 64, send_query, 0)

    pass_own(1)
    pass_near(0)
    pass_own(4)
    pass_near(1)
    pass_own(2)
    pass_near(4)
    pass_own(3)

    scale = (HD ** -0.5) * LOG2E
    own_order = order_s[own]
    is_own = lax.broadcasted_iota(jnp.int32, (8, HD), 0) == own
    for s in range(8):
        seen = jnp.sum(jnp.where(is_own, mask_in[:, s * HD:(s + 1) * HD], 0), 0, keepdims=True)
        ctx_bias[s:s + 1, :] = jnp.where(seen == 1, 0.0, NEG_FILL)

    def bias_of(x_):
        parts = []
        for c in range(2):
            s = x_ * 2 + c
            parts.append(ctx_bias[pl.ds(s, 1), :])
            visible = (order_s[s] < own_order) | (s == own)
            parts.append(jnp.full((1, 512), jnp.where(visible, 0.0, NEG_FILL), jnp.float32))
        return jnp.concatenate(parts, axis=1)

    def attend(state, x_):
        keys = kv[0, pl.ds(x_ * 2, 2)].reshape(1280, HD)
        values = kv[1, pl.ds(x_ * 2, 2)].reshape(1280, HD)
        scores = lax.dot_general(queries, keys, (((1,), (1,)), ((), ())), preferred_element_type=jnp.float32)
        scores = scores * scale + bias_of(x_)
        peak = jnp.max(scores, 1, keepdims=True)
        if state is not None:
            peak = jnp.maximum(state[0], peak)
        weights = jnp.exp2(scores - peak)
        total = weights[:, 0:HD]
        for t in range(1, 10):
            total = total + weights[:, t * HD:(t + 1) * HD]
        mixed = jnp.dot(weights.astype(jnp.bfloat16), values, preferred_element_type=jnp.float32)
        if state is not None:
            rescale = jnp.exp2(state[0] - peak)
            total = total + state[1] * rescale
            mixed = mixed + state[2] * rescale
        return peak, total, mixed

    def sibling_has_sent(kind):
        wait_for(kv.at[:, 0], sib_sem.at[kind])

    wait_for(q_rows, misc_sem.at[2])
    queries = q_rows[...].reshape(512, HD)
    sibling_has_sent(0)
    state = attend(None, x)
    pass_near(2)
    pass_near(3)
    sibling_has_sent(1)
    state = attend(state, left_x)
    for slot in (0, 1, 4, 2):
        pass_far(slot)
    sibling_has_sent(2)
    state = attend(state, right_x)
    pass_far(3)
    sibling_has_sent(3)
    _, total, mixed = attend(state, far_x)

    gate_copy.wait()
    step = step_s[own]
    gate = jnp.where(stays, gate_in[pl.ds(step, 1), :], gate_sib[pl.ds(step, 1), :])
    mixture = mixed / jnp.sum(total, 1, keepdims=True)
    out_rows[...] = (mixture * gate).astype(jnp.bfloat16).reshape(out_rows.shape)

    head = yh * 16 + z * 2 + yl
    dst = out_ref.at[:, pl.ds(pl.multiple_of(head * HD, HD), HD)]

    def send_back(j, carry):
        z_, yh_, k_ = (z + far_first(j // 8)) % 8, (yh + 2 + (j // 2) % 4) % 4, j % 2
        src = out_rows.at[yh_ * 16 + z_ * 2 + k_]
        here = stays & (yh_ == yh) & (z_ == z) & (k_ == k)

        @pl.when(here)
        def _():
            pltpu.make_async_copy(src, dst, misc_sem.at[3]).start()

        @pl.when(jnp.logical_not(here))
        def _():
            remote(src, dst, send_sem.at[5], misc_sem.at[3], device(x, yh_ * 2 + k, z_, k_)).start()

        return carry

    lax.fori_loop(0, 64, send_back, 0)

    wait_for(kv.at[:, pl.ds(0, 3)], send_sem.at[3])
    wait_for(kv.at[:, pl.ds(0, 4)], send_sem.at[4])

    @pl.when(stays)
    def _():
        wait_for(kv_out.at[pl.ds(0, 63)], send_sem.at[1])
        wait_for(q_rows.at[pl.ds(0, 63)], send_sem.at[2])
        wait_for(out_rows.at[pl.ds(0, 63)], send_sem.at[5])

    @pl.when(jnp.logical_not(stays))
    def _():
        wait_for(ctx_out, send_sem.at[0])
        wait_for(kv_out, send_sem.at[1])
        wait_for(q_rows, send_sem.at[2])
        wait_for(out_rows, send_sem.at[5])

    wait_for(out_rows, misc_sem.at[3])


def local(*args):
    bf16 = jnp.bfloat16
    any_space = pl.BlockSpec(memory_space=pl.ANY)
    dma = pltpu.SemaphoreType.DMA
    return pl.pallas_call(
        kernel,
        out_shape=jax.ShapeDtypeStruct((8, 8192), bf16),
        in_specs=[any_space] * 8,
        out_specs=pl.BlockSpec(memory_space=pltpu.VMEM),
        scratch_shapes=[
            pltpu.VMEM((8, 8192), bf16),
            pltpu.VMEM((8, 8192), bf16),
            pltpu.VMEM((8, 8192), bf16),
            pltpu.VMEM((2, 128, HD), bf16),
            pltpu.VMEM((64, HD), jnp.float32),
            pltpu.SMEM((8,), jnp.int32),
            pltpu.SMEM((8,), jnp.int32),
            pltpu.VMEM((8, 1024), jnp.int32),
            pltpu.VMEM((64, 2, 8, HD), bf16),
            pltpu.VMEM((2, 16, 8, HD), bf16),
            pltpu.VMEM((2, 8, 5, 16, 8, HD), bf16),
            pltpu.VMEM((64, 8, HD), bf16),
            pltpu.VMEM((64, HD), jnp.float32),
            pltpu.VMEM((64, 8, HD), bf16),
            pltpu.VMEM((8, 128), jnp.float32),
            dma((8,)),
            dma((5,)),
            dma((5,)),
            dma((5,)),
            dma((5, 2)),
            dma((4,)),
            dma((4,)),
            dma((6,)),
        ],
        compiler_params=pltpu.CompilerParams(
            collective_id=0, has_side_effects=True, vmem_limit_bytes=48 << 20
        ),
        cost_estimate=pl.CostEstimate(flops=1342177280, bytes_accessed=1 << 20, transcendentals=2621440),
        name="span_attention",
    )(*args)


def solution(mesh):
    rows = P(("span", "seq"), None)
    placed = (rows, rows, rows, P(None, "span", "seq"), P(None, "seq"), P(), P(), P())
    return jax.shard_map(local, mesh=mesh, in_specs=placed, out_specs=rows, check_vma=False)
```

```python
import jax
import jax.numpy as jnp
from jax import lax
from jax.experimental import pallas as pl
from jax.experimental.pallas import tpu as pltpu
from jax.sharding import PartitionSpec as P

MESH = pl.DeviceIdType.MESH
NEG_FILL = -1e30
LOG2E = 1.4426950408889634
HD = 128
Y_OFFSETS = (2, 1, 3, 0)
K_EARLY = (3, 1, 2, 0)
K_LATE = (3, 2, 1, 0)


def kernel(q_hbm, k_hbm, v_hbm, ctx_hbm, gate_hbm, order_hbm, step_hbm, mask_hbm, out_ref,
           q_in, k_in, v_in, ctx_in, gate_in, order_s, step_s, mask_in,
           kv_out, ctx_out, kv, q_rows, gate_sib, out_rows, ctx_bias,
           load_sem, own_sem, left_sem, right_sem, far_sem, sib_sem, misc_sem, send_sem,
           open_sem):
    span, seq = lax.axis_index("span"), lax.axis_index("seq")
    x, yl = span // 2, span % 2
    yh, z, k = seq // 16, (seq // 2) % 8, seq % 2
    y = yh * 2 + yl
    stays = yl == k
    own = x * 2 + k
    early = z < 4
    left_x, right_x, far_x = (x + 3) % 4, (x + 1) % 4, (x + 2) % 4

    def device(x_, y_, z_, k_):
        return (x_ * 2 + y_ % 2, (y_ // 2) * 16 + z_ * 2 + k_)

    left, right = device(left_x, y, z, k), device(right_x, y, z, k)
    sibling = device(x, y, z, 1 - k)

    def remote(src, dst, sent, got, to):
        return pltpu.make_async_remote_copy(
            src_ref=src, dst_ref=dst, send_sem=sent, recv_sem=got, device_id=to, device_id_type=MESH
        )

    def wait_for(ref, sem):
        pltpu.make_async_copy(ref, ref, sem).wait()

    def signal(sem, to):
        pl.semaphore_signal(sem, inc=1, device_id=to, device_id_type=MESH)

    barrier = pltpu.get_barrier_semaphore()
    hears = jnp.where(early, 0, 1)
    for b in (4, 5, 3, 7, 6, 2, 1, 0):
        for a in Y_OFFSETS:
            to = (x * 2 + k, (seq - k + hears) ^ (a * 16 + b * 2))
            if a or b:
                signal(barrier, to)
            else:
                @pl.when(jnp.logical_not(stays & (k == hears)))
                def _():
                    signal(barrier, to)

    for x_ in (left_x, right_x):
        signal(barrier, device(x_, y, z, 0))

    @pl.when(k == 1)
    def _():
        signal(barrier, sibling)

    loads = [
        pltpu.make_async_copy(src, dst, load_sem.at[i])
        for i, (src, dst) in enumerate(
            [(k_hbm, k_in), (v_hbm, v_in), (ctx_hbm, ctx_in), (q_hbm, q_in), (gate_hbm, gate_in),
             (order_hbm, order_s), (step_hbm, step_s), (mask_hbm, mask_in)]
        )
    ]
    for load in loads:
        load.start()

    for load in loads[:3]:
        load.wait()
    for h in range(64):
        kv_out[h, 0] = k_in[:, h * HD:(h + 1) * HD]
        kv_out[h, 1] = v_in[:, h * HD:(h + 1) * HD]
    ctx_out[...] = ctx_in[...].reshape(ctx_out.shape)
    for load in loads[3:]:
        load.wait()

    @pl.when(k == 0)
    def _():
        pl.semaphore_wait(barrier, 37 - (early & (yl == 0)).astype(jnp.int32))
        signal(open_sem, sibling)

    @pl.when(k == 1)
    def _():
        pl.semaphore_wait(open_sem, 1)

    def await_late_rows():
        @pl.when(k == 1)
        def _():
            pl.semaphore_wait(barrier, 32 - (jnp.logical_not(early) & (yl == 1)).astype(jnp.int32))
            signal(open_sem, sibling)

        @pl.when(k == 0)
        def _():
            pl.semaphore_wait(open_sem, 1)

    gate_copy = remote(gate_in, gate_sib, misc_sem.at[0], misc_sem.at[1], sibling)
    gate_copy.start()

    def send_context():
        @pl.when(stays)
        def _():
            pltpu.make_async_copy(ctx_out, kv.at[:, own, 0], own_sem.at[0]).start()

        @pl.when(jnp.logical_not(stays))
        def _():
            remote(ctx_out, kv.at[:, span, 0], send_sem.at[0], own_sem.at[0], device(x, yh * 2 + k, z, yl)).start()

    head = (seq - k) + yl

    def send(src_of, dst, sent, got, b, may_stay):
        for a in Y_OFFSETS:
            for al in (1, 0):
                to = head ^ (a * 16 + b * 2 + al)
                src = src_of(to)
                device_id = (span ^ al, head ^ (a * 16 + b * 2))
                if a or al or not may_stay:
                    remote(src, dst(a), sent, got, device_id).start()
                else:
                    here = stays & (b == 0)

                    @pl.when(here)
                    def _():
                        pltpu.make_async_copy(src, dst(a), got).start()

                    @pl.when(jnp.logical_not(here))
                    def _():
                        remote(src, dst(a), sent, got, device_id).start()

    def send_keys(b, may_stay):
        group = b // 2
        send(lambda h: kv_out.at[h], lambda a: kv.at[:, span, 1 + group, b % 2 * 8 + 2 * a + k],
             send_sem.at[1], own_sem.at[1 + group], b, may_stay)

    def send_queries(b, may_stay):
        send(lambda h: q_in.at[:, pl.ds(pl.multiple_of(h * HD, HD), HD)], lambda a: q_rows.at[b * 8 + 2 * a + k],
             send_sem.at[2], misc_sem.at[2], b, may_stay)

    to_early = jnp.where(early, 0, 4)
    to_late = 4 - to_early

    def to_sibling(ref, kind, slot):
        remote(ref, ref, send_sem.at[4], sib_sem.at[kind, slot // 4], sibling).start()

    def pass_own(slot):
        ref = kv.at[:, own, slot]
        wait_for(ref, own_sem.at[slot])
        remote(ref, ref, send_sem.at[3], left_sem.at[slot], right).start()
        remote(ref, ref, send_sem.at[3], right_sem.at[slot], left).start()
        to_sibling(ref, 0, slot)

    def pass_near(slot):
        from_left, from_right = kv.at[:, left_x * 2 + k, slot], kv.at[:, right_x * 2 + k, slot]
        wait_for(from_left, left_sem.at[slot])
        half = kv.at[0, left_x * 2 + k, slot]
        remote(half, half, send_sem.at[3], far_sem.at[slot, 0], right).start()
        to_sibling(from_left, 1, slot)
        wait_for(from_right, right_sem.at[slot])
        half = kv.at[1, right_x * 2 + k, slot]
        remote(half, half, send_sem.at[3], far_sem.at[slot, 1], left).start()
        to_sibling(from_right, 2, slot)

    def pass_far(slot):
        ref = kv.at[:, far_x * 2 + k, slot]
        wait_for(kv.at[0, far_x * 2 + k, slot], far_sem.at[slot, 0])
        wait_for(kv.at[1, far_x * 2 + k, slot], far_sem.at[slot, 1])
        to_sibling(ref, 3, slot)

    scale = (HD ** -0.5) * LOG2E
    own_order = order_s[own]
    is_own = lax.broadcasted_iota(jnp.int32, (8, HD), 0) == own
    for s in range(8):
        seen = jnp.sum(jnp.where(is_own, mask_in[:, s * HD:(s + 1) * HD], 0), 0, keepdims=True)
        ctx_bias[s:s + 1, :] = jnp.where(seen == 1, 0.0, NEG_FILL)

    def span_bias(s, n):
        visible = (order_s[s] < own_order) | (s == own)
        return jnp.full((1, n), jnp.where(visible, 0.0, NEG_FILL), jnp.float32)

    def attend(state, spans, groups, bias):
        keys = kv[0, spans, groups].reshape(1024, HD)
        values = kv[1, spans, groups].reshape(1024, HD)
        scores = lax.dot_general(queries, keys, (((1,), (1,)), ((), ())), preferred_element_type=jnp.float32)
        scores = scores * scale + bias
        peak = jnp.max(scores, 1, keepdims=True)
        if state is not None:
            peak = jnp.maximum(state[0], peak)
        weights = jnp.exp2(scores - peak)
        total = weights[:, 0:HD]
        for t in range(1, 8):
            total = total + weights[:, t * HD:(t + 1) * HD]
        mixed = jnp.dot(weights.astype(jnp.bfloat16), values, preferred_element_type=jnp.float32)
        if state is not None:
            rescale = jnp.exp2(state[0] - peak)
            total = total + state[1] * rescale
            mixed = mixed + state[2] * rescale
        return peak, total, mixed

    def attend_early(state, x_):
        parts = []
        for c in range(2):
            parts += [ctx_bias[pl.ds(x_ * 2 + c, 1), :], span_bias(x_ * 2 + c, 384)]
        return attend(state, pl.ds(x_ * 2, 2), slice(0, 4), jnp.concatenate(parts, axis=1))

    def attend_last(state):
        return attend(state, slice(0, 8), 4, jnp.concatenate([span_bias(s, 128) for s in range(8)], axis=1))

    def sibling_early(kind):
        wait_for(kv.at[:, 0, pl.ds(0, 4)], sib_sem.at[kind, 0])

    @pl.when(early)
    def _():
        send_context()

    for i in K_EARLY:
        send_keys(to_early + i, i == 0)
    await_late_rows()

    @pl.when(jnp.logical_not(early))
    def _():
        send_context()

    for i in K_LATE:
        send_keys(to_late + i, i == 0)
    for i in K_EARLY:
        send_queries(to_early + i, i == 0)
    for i in K_LATE:
        send_queries(to_late + i, i == 0)
    pass_own(0)
    pass_own(1)
    pass_own(2)
    pass_own(3)
    pass_own(4)
    pass_near(0)
    wait_for(q_rows, misc_sem.at[2])
    queries = q_rows[...].reshape(512, HD)
    sibling_early(0)
    state = attend_early(None, x)
    pass_near(1)
    pass_near(2)
    pass_near(3)
    sibling_early(1)
    state = attend_early(state, left_x)
    pass_near(4)
    pass_far(0)
    pass_far(1)
    sibling_early(2)
    state = attend_early(state, right_x)
    pass_far(2)
    pass_far(3)
    pass_far(4)
    sibling_early(3)
    state = attend_early(state, far_x)
    for kind in range(4):
        wait_for(kv.at[:, 0, 4], sib_sem.at[kind, 1])
    _, total, mixed = attend_last(state)

    gate_copy.wait()
    step = step_s[own]
    gate = jnp.where(stays, gate_in[pl.ds(step, 1), :], gate_sib[pl.ds(step, 1), :])
    mixture = mixed / jnp.sum(total, 1, keepdims=True)
    out_rows[...] = (mixture * gate).astype(jnp.bfloat16).reshape(out_rows.shape)

    dst = out_ref.at[:, pl.ds(pl.multiple_of(head * HD, HD), HD)]
    for b in (4, 5, 3, 7, 6, 2, 1, 0):
        for a in Y_OFFSETS:
            for k_ in range(2):
                src = out_rows.at[b * 8 + 2 * a + k_]
                to = (x * 2 + k, (seq - k + k_) ^ (a * 16 + b * 2))
                if a or b:
                    remote(src, dst, send_sem.at[5], misc_sem.at[3], to).start()
                else:
                    here = stays & (k == k_)

                    @pl.when(here)
                    def _():
                        pltpu.make_async_copy(src, dst, misc_sem.at[3]).start()

                    @pl.when(jnp.logical_not(here))
                    def _():
                        remote(src, dst, send_sem.at[5], misc_sem.at[3], to).start()

    wait_for(kv.at[:, pl.ds(0, 3)], send_sem.at[3])
    wait_for(kv.at[:, pl.ds(0, 4)], send_sem.at[4])

    @pl.when(stays)
    def _():
        wait_for(kv_out.at[pl.ds(0, 63)], send_sem.at[1])
        wait_for(q_rows.at[pl.ds(0, 63)], send_sem.at[2])
        wait_for(out_rows.at[pl.ds(0, 63)], send_sem.at[5])

    @pl.when(jnp.logical_not(stays))
    def _():
        wait_for(ctx_out, send_sem.at[0])
        wait_for(kv_out, send_sem.at[1])
        wait_for(q_rows, send_sem.at[2])
        wait_for(out_rows, send_sem.at[5])

    wait_for(out_rows, misc_sem.at[3])


def local(*args):
    bf16 = jnp.bfloat16
    in_hbm = pl.BlockSpec(memory_space=pltpu.HBM)
    dma = pltpu.SemaphoreType.DMA
    return pl.pallas_call(
        kernel,
        out_shape=jax.ShapeDtypeStruct((8, 8192), bf16),
        in_specs=[in_hbm] * 8,
        out_specs=pl.BlockSpec(memory_space=pltpu.VMEM),
        scratch_shapes=[
            pltpu.VMEM((8, 8192), bf16),
            pltpu.VMEM((8, 8192), bf16),
            pltpu.VMEM((8, 8192), bf16),
            pltpu.VMEM((2, 128, HD), bf16),
            pltpu.VMEM((64, HD), jnp.float32),
            pltpu.SMEM((8,), jnp.int32),
            pltpu.SMEM((8,), jnp.int32),
            pltpu.VMEM((8, 1024), jnp.int32),
            pltpu.VMEM((64, 2, 8, HD), bf16),
            pltpu.VMEM((2, 16, 8, HD), bf16),
            pltpu.VMEM((2, 8, 5, 16, 8, HD), bf16),
            pltpu.VMEM((64, 8, HD), bf16),
            pltpu.VMEM((64, HD), jnp.float32),
            pltpu.VMEM((64, 8, HD), bf16),
            pltpu.VMEM((8, 128), jnp.float32),
            dma((8,)),
            dma((5,)),
            dma((5,)),
            dma((5,)),
            dma((5, 2)),
            dma((4, 2)),
            dma((4,)),
            dma((6,)),
            pltpu.SemaphoreType.REGULAR,
        ],
        compiler_params=pltpu.CompilerParams(
            collective_id=0, has_side_effects=True, vmem_limit_bytes=60 << 20
        ),
        cost_estimate=pl.CostEstimate(flops=1342177280, bytes_accessed=1 << 20, transcendentals=2621440),
        name="span_attention",
    )(*args)


def solution(mesh):
    rows = P(("span", "seq"), None)
    placed = (rows, rows, rows, P(None, "span", "seq"), P(None, "seq"), P(), P(), P())
    return jax.shard_map(local, mesh=mesh, in_specs=placed, out_specs=rows, check_vma=False)
```

```python
import jax
import jax.numpy as jnp
from jax import lax
from jax.experimental import pallas as pl
from jax.experimental.pallas import tpu as pltpu
from jax.sharding import PartitionSpec as P

MESH = pl.DeviceIdType.MESH
NEG_FILL = -1e30
LOG2E = 1.4426950408889634
HD = 128
Y_OFFSETS = (2, 1, 3, 0)
FIRST = 2


def kernel(q_hbm, k_hbm, v_hbm, ctx_hbm, gate_hbm, order_hbm, step_hbm, mask_hbm, out_ref,
           q_in, k_in, v_in, ctx_in, gate_in, order_s, step_s, mask_in,
           qkv_out, ctx_out, mine, kv, gate_sib, out_rows, ctx_bias,
           load_sem, own_sem, left_sem, right_sem, far_sem, sib_sem, here_sem, misc_sem, send_sem,
           open_sem):
    span, seq = lax.axis_index("span"), lax.axis_index("seq")
    x, yl = span // 2, span % 2
    yh, z, k = seq // 16, (seq // 2) % 8, seq % 2
    y = yh * 2 + yl
    stays = yl == k
    own = x * 2 + k
    early = z < 4
    left_x, right_x, far_x = (x + 3) % 4, (x + 1) % 4, (x + 2) % 4

    def device(x_, y_, z_, k_):
        return (x_ * 2 + y_ % 2, (y_ // 2) * 16 + z_ * 2 + k_)

    left, right = device(left_x, y, z, k), device(right_x, y, z, k)
    sibling = device(x, y, z, 1 - k)

    def remote(src, dst, sent, got, to):
        return pltpu.make_async_remote_copy(
            src_ref=src, dst_ref=dst, send_sem=sent, recv_sem=got, device_id=to, device_id_type=MESH
        )

    def wait_for(ref, sem):
        pltpu.make_async_copy(ref, ref, sem).wait()

    def signal(sem, to):
        pl.semaphore_signal(sem, inc=1, device_id=to, device_id_type=MESH)

    barrier = pltpu.get_barrier_semaphore()
    hears = jnp.where(early, 0, 1)
    for b in (4, 5, 3, 7, 6, 2, 1, 0):
        for a in Y_OFFSETS:
            to = (x * 2 + k, (seq - k + hears) ^ (a * 16 + b * 2))
            if a or b:
                signal(barrier, to)
            else:
                @pl.when(jnp.logical_not(stays & (k == hears)))
                def _():
                    signal(barrier, to)

    for x_ in (left_x, right_x):
        signal(barrier, device(x_, y, z, 0))

    @pl.when(k == 1)
    def _():
        signal(barrier, sibling)

    loads = [
        pltpu.make_async_copy(src, dst, load_sem.at[i])
        for i, (src, dst) in enumerate(
            [(k_hbm, k_in), (v_hbm, v_in), (q_hbm, q_in), (ctx_hbm, ctx_in), (gate_hbm, gate_in),
             (order_hbm, order_s), (step_hbm, step_s), (mask_hbm, mask_in)]
        )
    ]
    for load in loads:
        load.start()

    for load in loads[:4]:
        load.wait()
    for h in range(64):
        for t, ref in enumerate((k_in, v_in, q_in)):
            qkv_out[h, t] = ref[:, h * HD:(h + 1) * HD]
    for t in range(2):
        ctx_out[:, t] = ctx_in[t].reshape(16, 8, HD)
    for load in loads[4:]:
        load.wait()

    @pl.when(k == 0)
    def _():
        pl.semaphore_wait(barrier, 37 - (early & (yl == 0)).astype(jnp.int32))
        signal(open_sem, sibling)

    @pl.when(k == 1)
    def _():
        pl.semaphore_wait(open_sem, 1)

    def await_late_rows():
        @pl.when(k == 1)
        def _():
            pl.semaphore_wait(barrier, 32 - (jnp.logical_not(early) & (yl == 1)).astype(jnp.int32))
            signal(open_sem, sibling)

        @pl.when(k == 0)
        def _():
            pl.semaphore_wait(open_sem, 1)

    gate_copy = remote(gate_in, gate_sib, misc_sem.at[0], misc_sem.at[1], sibling)
    gate_copy.start()

    def send_context():
        @pl.when(stays)
        def _():
            pltpu.make_async_copy(ctx_out, kv.at[own, 0], own_sem.at[0]).start()

        @pl.when(jnp.logical_not(stays))
        def _():
            remote(ctx_out, kv.at[span, 0], send_sem.at[0], own_sem.at[0], device(x, yh * 2 + k, z, yl)).start()

    head = (seq - k) + yl

    def send(b, may_stay):
        got = own_sem.at[1 + b // 2]
        for a in Y_OFFSETS:
            dst = mine.at[b // 2, b % 2 * 8 + 2 * a + k]
            for al in (1, 0):
                src = qkv_out.at[head ^ (a * 16 + b * 2 + al)]
                device_id = (span ^ al, head ^ (a * 16 + b * 2))
                if a or al or not may_stay:
                    remote(src, dst, send_sem.at[1], got, device_id).start()
                else:
                    here = stays & (b == 0)

                    @pl.when(here)
                    def _():
                        pltpu.make_async_copy(src, dst, got).start()

                    @pl.when(jnp.logical_not(here))
                    def _():
                        remote(src, dst, send_sem.at[1], got, device_id).start()

    to_early = jnp.where(early, 0, 4)
    to_late = 4 - to_early

    def to_sibling(src, s, slot, kind):
        remote(src, kv.at[s, slot], send_sem.at[4], sib_sem.at[kind, int(slot >= FIRST)], sibling).start()

    def pass_own(slot):
        dst = kv.at[own, slot]
        if slot:
            wait_for(mine.at[slot - 1], own_sem.at[slot])
            src = mine.at[slot - 1, :, pl.ds(0, 2)]
            pltpu.make_async_copy(src, dst, here_sem.at[int(slot >= FIRST)]).start()
        else:
            wait_for(dst, own_sem.at[slot])
            src = dst
        remote(src, dst, send_sem.at[3], left_sem.at[slot], right).start()
        remote(src, dst, send_sem.at[3], right_sem.at[slot], left).start()
        to_sibling(src, own, slot, 0)

    def pass_near(slot):
        for t, (x_, got, to) in enumerate(((left_x, left_sem, right), (right_x, right_sem, left))):
            s = x_ * 2 + k
            wait_for(kv.at[s, slot], got.at[slot])
            half = kv.at[s, slot, :, t]
            remote(half, half, send_sem.at[3], far_sem.at[slot, t], to).start()
            to_sibling(kv.at[s, slot], s, slot, 1 + t)

    def pass_far(slot):
        s = far_x * 2 + k
        for t in range(2):
            wait_for(kv.at[s, slot, :, t], far_sem.at[slot, t])
        to_sibling(kv.at[s, slot], s, slot, 3)

    scale = (HD ** -0.5) * LOG2E
    own_order = order_s[own]
    is_own = lax.broadcasted_iota(jnp.int32, (8, HD), 0) == own
    for s in range(8):
        seen = jnp.sum(jnp.where(is_own, mask_in[:, s * HD:(s + 1) * HD], 0), 0, keepdims=True)
        ctx_bias[s:s + 1, :] = jnp.where(seen == 1, 0.0, NEG_FILL)

    def span_bias(s, n):
        visible = (order_s[s] < own_order) | (s == own)
        return jnp.full((1, n), jnp.where(visible, 0.0, NEG_FILL), jnp.float32)

    def attend(state, x_, groups, bias):
        spans = pl.ds(x_ * 2, 2)
        keys = kv[spans, groups, :, 0].reshape(bias.shape[1], HD)
        values = kv[spans, groups, :, 1].reshape(bias.shape[1], HD)
        scores = lax.dot_general(queries, keys, (((1,), (1,)), ((), ())), preferred_element_type=jnp.float32)
        scores = scores * scale + bias
        peak = jnp.max(scores, 1, keepdims=True)
        if state is not None:
            peak = jnp.maximum(state[0], peak)
        weights = jnp.exp2(scores - peak)
        total = weights[:, 0:HD]
        for t in range(1, bias.shape[1] // HD):
            total = total + weights[:, t * HD:(t + 1) * HD]
        mixed = jnp.dot(weights.astype(jnp.bfloat16), values, preferred_element_type=jnp.float32)
        if state is not None:
            rescale = jnp.exp2(state[0] - peak)
            total = total + state[1] * rescale
            mixed = mixed + state[2] * rescale
        return peak, total, mixed

    def attend_first(state, kind, x_):
        wait_for(kv.at[0, pl.ds(0, FIRST)], sib_sem.at[kind, 0])
        parts = []
        for c in range(2):
            parts += [ctx_bias[pl.ds(x_ * 2 + c, 1), :], span_bias(x_ * 2 + c, (FIRST - 1) * 128)]
        return attend(state, x_, slice(0, FIRST), jnp.concatenate(parts, axis=1))

    def attend_rest(state, kind, x_):
        wait_for(kv.at[0, pl.ds(FIRST, 5 - FIRST)], sib_sem.at[kind, 1])
        parts = [span_bias(x_ * 2 + c, (5 - FIRST) * 128) for c in range(2)]
        return attend(state, x_, slice(FIRST, 5), jnp.concatenate(parts, axis=1))

    @pl.when(early)
    def _():
        send_context()


    @pl.when(early)
    def _():
        for i in (3, 2, 1, 0):
            send(to_early + i, i == 0)


    @pl.when(jnp.logical_not(early))
    def _():
        for i in (0,):
            send(to_early + i, False)

    await_late_rows()

    @pl.when(jnp.logical_not(early))
    def _():
        send_context()

    for i in (0, 1, 2, 3):
        send(to_late + i, i == 0)

    @pl.when(jnp.logical_not(early))
    def _():
        for i in (1, 3, 2):
            send(to_early + i, False)

    pass_own(0)
    pass_own(1)
    pass_near(0)
    pass_own(2)
    pass_own(3)
    pass_own(4)
    pass_near(1)
    queries = mine[:, :, 2].reshape(512, HD)
    wait_for(kv.at[0, pl.ds(0, FIRST - 1)], here_sem.at[0])
    wait_for(kv.at[0, pl.ds(0, 5 - FIRST)], here_sem.at[1])
    state = attend_first(None, 0, x)
    state = attend_first(state, 1, left_x)
    pass_near(2)
    pass_near(3)
    pass_near(4)
    state = attend_rest(state, 0, x)
    pass_far(0)
    pass_far(1)
    pass_far(2)
    state = attend_first(state, 2, right_x)
    state = attend_first(state, 3, far_x)
    pass_far(3)
    pass_far(4)
    state = attend_rest(state, 1, left_x)
    state = attend_rest(state, 2, right_x)
    state = attend_rest(state, 3, far_x)
    _, total, mixed = state

    gate_copy.wait()
    step = step_s[own]
    gate = jnp.where(stays, gate_in[pl.ds(step, 1), :], gate_sib[pl.ds(step, 1), :])
    mixture = mixed / jnp.sum(total, 1, keepdims=True)
    out_rows[...] = (mixture * gate).astype(jnp.bfloat16).reshape(out_rows.shape)

    dst = out_ref.at[:, pl.ds(pl.multiple_of(head * HD, HD), HD)]
    for b in (4, 5, 3, 7, 6, 2, 1, 0):
        for a in Y_OFFSETS:
            for k_ in range(2):
                src = out_rows.at[b * 8 + 2 * a + k_]
                to = (x * 2 + k, (seq - k + k_) ^ (a * 16 + b * 2))
                if a or b:
                    remote(src, dst, send_sem.at[5], misc_sem.at[3], to).start()
                else:
                    here = stays & (k == k_)

                    @pl.when(here)
                    def _():
                        pltpu.make_async_copy(src, dst, misc_sem.at[3]).start()

                    @pl.when(jnp.logical_not(here))
                    def _():
                        remote(src, dst, send_sem.at[5], misc_sem.at[3], to).start()

    wait_for(kv.at[pl.ds(0, 3)], send_sem.at[3])
    wait_for(kv.at[pl.ds(0, 4)], send_sem.at[4])

    @pl.when(stays)
    def _():
        wait_for(qkv_out.at[pl.ds(0, 63)], send_sem.at[1])
        wait_for(out_rows.at[pl.ds(0, 63)], send_sem.at[5])

    @pl.when(jnp.logical_not(stays))
    def _():
        wait_for(ctx_out, send_sem.at[0])
        wait_for(qkv_out, send_sem.at[1])
        wait_for(out_rows, send_sem.at[5])

    wait_for(out_rows, misc_sem.at[3])


def local(*args):
    bf16 = jnp.bfloat16
    in_hbm = pl.BlockSpec(memory_space=pltpu.HBM)
    dma = pltpu.SemaphoreType.DMA
    return pl.pallas_call(
        kernel,
        out_shape=jax.ShapeDtypeStruct((8, 8192), bf16),
        in_specs=[in_hbm] * 8,
        out_specs=pl.BlockSpec(memory_space=pltpu.HBM),
        scratch_shapes=[
            pltpu.VMEM((8, 8192), bf16),
            pltpu.VMEM((8, 8192), bf16),
            pltpu.VMEM((8, 8192), bf16),
            pltpu.VMEM((2, 128, HD), bf16),
            pltpu.VMEM((64, HD), jnp.float32),
            pltpu.SMEM((8,), jnp.int32),
            pltpu.SMEM((8,), jnp.int32),
            pltpu.VMEM((8, 1024), jnp.int32),
            pltpu.VMEM((64, 3, 8, HD), bf16),
            pltpu.VMEM((16, 2, 8, HD), bf16),
            pltpu.VMEM((4, 16, 3, 8, HD), bf16),
            pltpu.VMEM((8, 5, 16, 2, 8, HD), bf16),
            pltpu.VMEM((64, HD), jnp.float32),
            pltpu.VMEM((64, 8, HD), bf16),
            pltpu.VMEM((8, 128), jnp.float32),
            dma((8,)),
            dma((5,)),
            dma((5,)),
            dma((5,)),
            dma((5, 2)),
            dma((4, 2)),
            dma((2,)),
            dma((4,)),
            dma((6,)),
            pltpu.SemaphoreType.REGULAR,
        ],
        compiler_params=pltpu.CompilerParams(
            collective_id=0, has_side_effects=True, vmem_limit_bytes=60 << 20
        ),
        cost_estimate=pl.CostEstimate(flops=1342177280, bytes_accessed=1 << 20, transcendentals=2621440),
        name="span_attention",
    )(*args)


def solution(mesh):
    rows = P(("span", "seq"), None)
    placed = (rows, rows, rows, P(None, "span", "seq"), P(None, "seq"), P(), P(), P())
    return jax.shard_map(local, mesh=mesh, in_specs=placed, out_specs=rows, check_vma=False)
```

```python
import jax
import jax.numpy as jnp
from jax import lax
from jax.experimental import pallas as pl
from jax.experimental.pallas import tpu as pltpu
from jax.sharding import PartitionSpec as P

MESH = pl.DeviceIdType.MESH
NEG_FILL = -1e30
LOG2E = 1.4426950408889634
HD = 128
Y_OFFSETS = (2, 1, 3, 0)
FIRST = 2


def kernel(q_hbm, k_hbm, v_hbm, ctx_hbm, gate_hbm, order_hbm, step_hbm, mask_hbm, out_ref,
           q_in, k_in, v_in, ctx_in, gate_in, order_s, step_s, mask_in,
           qkv_out, ctx_out, mine, kv, gate_sib, out_rows, ctx_bias,
           load_sem, own_sem, left_sem, right_sem, far_sem, sib_sem, here_sem, misc_sem, send_sem,
           open_sem):
    span, seq = lax.axis_index("span"), lax.axis_index("seq")
    x, yl = span // 2, span % 2
    yh, z, k = seq // 16, (seq // 2) % 8, seq % 2
    y = yh * 2 + yl
    stays = yl == k
    own = x * 2 + k
    early = z < 4
    left_x, right_x, far_x = (x + 3) % 4, (x + 1) % 4, (x + 2) % 4

    def device(x_, y_, z_, k_):
        return (x_ * 2 + y_ % 2, (y_ // 2) * 16 + z_ * 2 + k_)

    left, right = device(left_x, y, z, k), device(right_x, y, z, k)
    sibling = device(x, y, z, 1 - k)

    def remote(src, dst, sent, got, to):
        return pltpu.make_async_remote_copy(
            src_ref=src, dst_ref=dst, send_sem=sent, recv_sem=got, device_id=to, device_id_type=MESH
        )

    def wait_for(ref, sem):
        pltpu.make_async_copy(ref, ref, sem).wait()

    def signal(sem, to):
        pl.semaphore_signal(sem, inc=1, device_id=to, device_id_type=MESH)

    barrier = pltpu.get_barrier_semaphore()
    hears = jnp.where(early, 0, 1)
    for b in (4, 5, 3, 7, 6, 2, 1, 0):
        for a in Y_OFFSETS:
            to = (x * 2 + k, (seq - k + hears) ^ (a * 16 + b * 2))
            if a or b:
                signal(barrier, to)
            else:
                @pl.when(jnp.logical_not(stays & (k == hears)))
                def _():
                    signal(barrier, to)

    for x_ in (left_x, right_x):
        signal(barrier, device(x_, y, z, 0))

    @pl.when(k == 1)
    def _():
        signal(barrier, sibling)

    loads = [
        pltpu.make_async_copy(src, dst, load_sem.at[i])
        for i, (src, dst) in enumerate(
            [(k_hbm, k_in), (v_hbm, v_in), (q_hbm, q_in), (ctx_hbm, ctx_in), (gate_hbm, gate_in),
             (order_hbm, order_s), (step_hbm, step_s), (mask_hbm, mask_in)]
        )
    ]
    for load in loads:
        load.start()

    for load in loads[:4]:
        load.wait()
    for h in range(64):
        for t, ref in enumerate((k_in, v_in, q_in)):
            qkv_out[h, t] = ref[:, h * HD:(h + 1) * HD]
    for t in range(2):
        ctx_out[:, t] = ctx_in[t].reshape(16, 8, HD)
    for load in loads[4:]:
        load.wait()

    @pl.when(k == 0)
    def _():
        pl.semaphore_wait(barrier, 37 - (early & (yl == 0)).astype(jnp.int32))
        signal(open_sem, sibling)

    @pl.when(k == 1)
    def _():
        pl.semaphore_wait(open_sem, 1)

    def await_late_rows():
        @pl.when(k == 1)
        def _():
            pl.semaphore_wait(barrier, 32 - (jnp.logical_not(early) & (yl == 1)).astype(jnp.int32))
            signal(open_sem, sibling)

        @pl.when(k == 0)
        def _():
            pl.semaphore_wait(open_sem, 1)

    gate_copy = remote(gate_in, gate_sib, misc_sem.at[0], misc_sem.at[1], sibling)
    gate_copy.start()

    def send_context():
        @pl.when(stays)
        def _():
            pltpu.make_async_copy(ctx_out, kv.at[own, 0], own_sem.at[0]).start()

        @pl.when(jnp.logical_not(stays))
        def _():
            remote(ctx_out, kv.at[span, 0], send_sem.at[0], own_sem.at[0], device(x, yh * 2 + k, z, yl)).start()

    head = (seq - k) + yl

    def send(b, may_stay):
        got = own_sem.at[1 + b // 2]
        for a in Y_OFFSETS:
            dst = mine.at[b // 2, b % 2 * 8 + 2 * a + k]
            for al in (1, 0):
                src = qkv_out.at[head ^ (a * 16 + b * 2 + al)]
                device_id = (span ^ al, head ^ (a * 16 + b * 2))
                if a or al or not may_stay:
                    remote(src, dst, send_sem.at[1], got, device_id).start()
                else:
                    here = stays & (b == 0)

                    @pl.when(here)
                    def _():
                        pltpu.make_async_copy(src, dst, got).start()

                    @pl.when(jnp.logical_not(here))
                    def _():
                        remote(src, dst, send_sem.at[1], got, device_id).start()

    to_early = jnp.where(early, 0, 4)
    to_late = 4 - to_early

    def to_sibling(src, s, slot, kind):
        remote(src, kv.at[s, slot], send_sem.at[4], sib_sem.at[kind, int(slot >= FIRST)], sibling).start()

    def pass_own(slot):
        dst = kv.at[own, slot]
        if slot:
            wait_for(mine.at[slot - 1], own_sem.at[slot])
            src = mine.at[slot - 1, :, pl.ds(0, 2)]
            pltpu.make_async_copy(src, dst, here_sem.at[int(slot >= FIRST)]).start()
        else:
            wait_for(dst, own_sem.at[slot])
            src = dst
        remote(src, dst, send_sem.at[3], left_sem.at[slot], right).start()
        remote(src, dst, send_sem.at[3], right_sem.at[slot], left).start()
        to_sibling(src, own, slot, 0)

    def pass_near(slot):
        for t, (x_, got, to) in enumerate(((left_x, left_sem, right), (right_x, right_sem, left))):
            s = x_ * 2 + k
            wait_for(kv.at[s, slot], got.at[slot])
            half = kv.at[s, slot, :, t]
            remote(half, half, send_sem.at[3], far_sem.at[slot, t], to).start()
            to_sibling(kv.at[s, slot], s, slot, 1 + t)

    def pass_far(slot):
        s = far_x * 2 + k
        for t in range(2):
            wait_for(kv.at[s, slot, :, t], far_sem.at[slot, t])
        to_sibling(kv.at[s, slot], s, slot, 3)

    scale = (HD ** -0.5) * LOG2E
    own_order = order_s[own]
    is_own = lax.broadcasted_iota(jnp.int32, (8, HD), 0) == own
    for s in range(8):
        seen = jnp.sum(jnp.where(is_own, mask_in[:, s * HD:(s + 1) * HD], 0), 0, keepdims=True)
        ctx_bias[s:s + 1, :] = jnp.where(seen == 1, 0.0, NEG_FILL)

    def span_bias(s, n):
        visible = (order_s[s] < own_order) | (s == own)
        return jnp.full((1, n), jnp.where(visible, 0.0, NEG_FILL), jnp.float32)

    def attend(state, x_, groups, bias):
        spans = pl.ds(x_ * 2, 2)
        keys = kv[spans, groups, :, 0].reshape(bias.shape[1], HD)
        values = kv[spans, groups, :, 1].reshape(bias.shape[1], HD)
        scores = lax.dot_general(queries, keys, (((1,), (1,)), ((), ())), preferred_element_type=jnp.float32)
        scores = scores * scale + bias
        peak = jnp.max(scores, 1, keepdims=True)
        if state is not None:
            peak = jnp.maximum(state[0], peak)
        weights = jnp.exp2(scores - peak)
        total = weights[:, 0:HD]
        for t in range(1, bias.shape[1] // HD):
            total = total + weights[:, t * HD:(t + 1) * HD]
        mixed = jnp.dot(weights.astype(jnp.bfloat16), values, preferred_element_type=jnp.float32)
        if state is not None:
            rescale = jnp.exp2(state[0] - peak)
            total = total + state[1] * rescale
            mixed = mixed + state[2] * rescale
        return peak, total, mixed

    def attend_first(state, kind, x_):
        wait_for(kv.at[0, pl.ds(0, FIRST)], sib_sem.at[kind, 0])
        parts = []
        for c in range(2):
            parts += [ctx_bias[pl.ds(x_ * 2 + c, 1), :], span_bias(x_ * 2 + c, (FIRST - 1) * 128)]
        return attend(state, x_, slice(0, FIRST), jnp.concatenate(parts, axis=1))

    def attend_rest(state, kind, x_):
        wait_for(kv.at[0, pl.ds(FIRST, 5 - FIRST)], sib_sem.at[kind, 1])
        parts = [span_bias(x_ * 2 + c, (5 - FIRST) * 128) for c in range(2)]
        return attend(state, x_, slice(FIRST, 5), jnp.concatenate(parts, axis=1))

    @pl.when(early)
    def _():
        send_context()


    @pl.when(early)
    def _():
        for i in (3, 2, 1, 0):
            send(to_early + i, i == 0)


    @pl.when(jnp.logical_not(early))
    def _():
        for i in (0,):
            send(to_early + i, False)

    await_late_rows()

    @pl.when(jnp.logical_not(early))
    def _():
        send_context()

    for i in (0, 1, 2, 3):
        send(to_late + i, i == 0)

    @pl.when(jnp.logical_not(early))
    def _():
        for i in (1, 3, 2):
            send(to_early + i, False)

    pass_own(0)
    pass_own(1)
    pass_near(0)
    pass_own(2)
    pass_own(3)
    pass_own(4)
    pass_near(1)
    queries = mine[:, :, 2].reshape(512, HD)
    wait_for(kv.at[0, pl.ds(0, FIRST - 1)], here_sem.at[0])
    wait_for(kv.at[0, pl.ds(0, 5 - FIRST)], here_sem.at[1])
    state = attend_first(None, 0, x)
    state = attend_first(state, 1, left_x)
    pass_near(2)
    pass_near(3)
    pass_near(4)
    state = attend_rest(state, 0, x)
    pass_far(0)
    pass_far(1)
    pass_far(2)
    state = attend_first(state, 2, right_x)
    state = attend_first(state, 3, far_x)
    pass_far(3)
    pass_far(4)
    state = attend_rest(state, 1, left_x)
    state = attend_rest(state, 2, right_x)
    state = attend_rest(state, 3, far_x)
    _, total, mixed = state

    gate_copy.wait()
    step = step_s[own]
    gate = jnp.where(stays, gate_in[pl.ds(step, 1), :], gate_sib[pl.ds(step, 1), :])

    dst = out_ref.at[:, pl.ds(pl.multiple_of(head * HD, HD), HD)]
    for b in (4, 5, 3, 7, 6, 2, 1, 0):
        rows = slice(b * 64, (b + 1) * 64)
        mixture = mixed[rows] / jnp.sum(total[rows], 1, keepdims=True)
        out_rows[b * 8:(b + 1) * 8] = (mixture * gate).astype(jnp.bfloat16).reshape(8, 8, HD)
        for a in Y_OFFSETS:
            for k_ in range(2):
                src = out_rows.at[b * 8 + 2 * a + k_]
                to = (x * 2 + k, (seq - k + k_) ^ (a * 16 + b * 2))
                if a or b:
                    remote(src, dst, send_sem.at[5], misc_sem.at[3], to).start()
                else:
                    here = stays & (k == k_)

                    @pl.when(here)
                    def _():
                        pltpu.make_async_copy(src, dst, misc_sem.at[3]).start()

                    @pl.when(jnp.logical_not(here))
                    def _():
                        remote(src, dst, send_sem.at[5], misc_sem.at[3], to).start()

    wait_for(kv.at[pl.ds(0, 3)], send_sem.at[3])
    wait_for(kv.at[pl.ds(0, 4)], send_sem.at[4])

    @pl.when(stays)
    def _():
        wait_for(qkv_out.at[pl.ds(0, 63)], send_sem.at[1])
        wait_for(out_rows.at[pl.ds(0, 63)], send_sem.at[5])

    @pl.when(jnp.logical_not(stays))
    def _():
        wait_for(ctx_out, send_sem.at[0])
        wait_for(qkv_out, send_sem.at[1])
        wait_for(out_rows, send_sem.at[5])

    wait_for(out_rows, misc_sem.at[3])


def local(*args):
    bf16 = jnp.bfloat16
    in_hbm = pl.BlockSpec(memory_space=pltpu.HBM)
    dma = pltpu.SemaphoreType.DMA
    return pl.pallas_call(
        kernel,
        out_shape=jax.ShapeDtypeStruct((8, 8192), bf16),
        in_specs=[in_hbm] * 8,
        out_specs=pl.BlockSpec(memory_space=pltpu.HBM),
        scratch_shapes=[
            pltpu.VMEM((8, 8192), bf16),
            pltpu.VMEM((8, 8192), bf16),
            pltpu.VMEM((8, 8192), bf16),
            pltpu.VMEM((2, 128, HD), bf16),
            pltpu.VMEM((64, HD), jnp.float32),
            pltpu.SMEM((8,), jnp.int32),
            pltpu.SMEM((8,), jnp.int32),
            pltpu.VMEM((8, 1024), jnp.int32),
            pltpu.VMEM((64, 3, 8, HD), bf16),
            pltpu.VMEM((16, 2, 8, HD), bf16),
            pltpu.VMEM((4, 16, 3, 8, HD), bf16),
            pltpu.VMEM((8, 5, 16, 2, 8, HD), bf16),
            pltpu.VMEM((64, HD), jnp.float32),
            pltpu.VMEM((64, 8, HD), bf16),
            pltpu.VMEM((8, 128), jnp.float32),
            dma((8,)),
            dma((5,)),
            dma((5,)),
            dma((5,)),
            dma((5, 2)),
            dma((4, 2)),
            dma((2,)),
            dma((4,)),
            dma((6,)),
            pltpu.SemaphoreType.REGULAR,
        ],
        compiler_params=pltpu.CompilerParams(
            collective_id=0, has_side_effects=True, vmem_limit_bytes=60 << 20
        ),
        cost_estimate=pl.CostEstimate(flops=1342177280, bytes_accessed=1 << 20, transcendentals=2621440),
        name="span_attention",
    )(*args)


def solution(mesh):
    rows = P(("span", "seq"), None)
    placed = (rows, rows, rows, P(None, "span", "seq"), P(None, "seq"), P(), P(), P())
    return jax.shard_map(local, mesh=mesh, in_specs=placed, out_specs=rows, check_vma=False)
```
